32 devices in a mesh: tm: 16 (over z, y, x), chan: 2 (over core).
Axes of the slice: x: 2, y: 2, z: 4, core: 2. Of those that a mesh axis runs over, the one named last changes fastest.
Arguments:
- field: float32 [2, 2, 64, 16384], P(None, None, 'chan', 'tm'), may hold values from -15.5 to 15.5
- noise: float32 [1, 2, 2, 64, 16384], P(None, None, None, 'chan', 'tm'), may hold values from -1.25 to 1.25
- assign: int32 [64], P('chan'), may hold values from 0 to 63, each once
Outputs:
- received: float32 [2, 2, 64, 16384], P(None, None, 'chan', 'tm')
- recovered: float32 [2, 2, 64, 16384], P(None, None, 'chan', 'tm')
The draws below stay inside these ranges and needn't reach their ends.
All inputs are finite; a program needn't handle non-finite values.
Results may differ from the reference program's by a relative error of at most 0.0003.
Values sent between devices are 32-bit elements; how exact they have to be, the bound alone decides.
A program may use at most 64 MiB of HBM per device.

```python
import jax
import jax.numpy as jnp
from jax import lax

OPTICAL_CHANNELS = 64
FILTER_HALF_TAPS = 128
STEPS = 2
FIBER_SECTIONS = 1
TIME_SAMPLES = 16384


def draw_field(key, part):
    reference_seed = jax.random.fold_in(key, 0)
    optical_tone_seed = jax.random.fold_in(key, 3)
    shape = (2, 2, OPTICAL_CHANNELS, TIME_SAMPLES)
    ramp = jnp.arange(TIME_SAMPLES, dtype=jnp.int32).astype(jnp.float32) / (TIME_SAMPLES - 1)
    optical_angle_offset = jax.random.uniform(optical_tone_seed, (2, 1, OPTICAL_CHANNELS, 1), jnp.float32, -3.1415927, 3.1415927)
    optical_tone = jnp.concatenate([jnp.cos(optical_angle_offset), jnp.sin(optical_angle_offset)], axis=1)
    reference_signal = jnp.clip(jax.random.normal(reference_seed, shape, jnp.float32), -4.0, 4.0)
    symbol_profile = jnp.sqrt(1.0 + 2.0 * ramp)
    return (0.5 * reference_signal * symbol_profile + 0.4 * optical_tone).astype(jnp.float32)


def draw_noise(key, part):
    rough_key, angle_seed = jax.random.split(key, 2)
    shape = (FIBER_SECTIONS, 2, 2, OPTICAL_CHANNELS, TIME_SAMPLES)
    optical_angle_offset = jax.random.uniform(angle_seed, (FIBER_SECTIONS, 2, 1, OPTICAL_CHANNELS, 1), jnp.float32, -3.1415927, 3.1415927)
    direction_vector = jnp.concatenate([jnp.cos(optical_angle_offset), jnp.sin(optical_angle_offset)], axis=2)
    rough = 0.15 * jnp.clip(jax.random.normal(rough_key, shape, jnp.float32), -6.0, 6.0)
    return (rough + 0.3 * direction_vector).astype(jnp.float32)


def setup_inputs(seed: int = 0) -> dict:
    key_list = jax.random.split(jax.random.key(seed), 4)
    return {
        "field": draw_field(jax.random.fold_in(key_list[3], 71), 0),
        "noise": draw_noise(jax.random.fold_in(key_list[3], 71), 0),
        "assign": jax.random.permutation(key_list[2], OPTICAL_CHANNELS).astype(jnp.int32),
    }


ATT = 0.955
GAMMA = 0.004
WALK = 0.5
SPREAD = 0.4
CHIRP = 0.25
EPS = 1e-06

def tap_tables(channel_ids, sign, reach, channels):
    rows = jnp.arange(3 * reach, dtype=jnp.int32)[:, None]
    cols = jnp.arange(reach, dtype=jnp.int32)[None, :]
    lag = cols - rows + reach
    interior_part = (jnp.abs(lag) <= reach).astype(jnp.float32)
    centre = WALK * reach * (2.0 * channel_ids.astype(jnp.float32) - (channels - 1)) / (channels - 1)
    centre = centre[:, None, None]
    width = SPREAD * reach
    offset = sign * lag.astype(jnp.float32)[None] - centre
    symbol_profile = jnp.exp(-jnp.square(offset / width))
    turn = jnp.square(offset) / (2.0 * CHIRP * reach)
    taps = jnp.arange(-reach, reach + 1, dtype=jnp.int32).astype(jnp.float32)
    scale = jnp.sqrt(lax.optimization_barrier(jnp.sum(jnp.exp(-2.0 * jnp.square((taps[None, :] - centre[:, :, 0]) / width)), axis=1)))
    scale = scale[:, None, None]
    mat_re = interior_part * symbol_profile * jnp.cos(turn) / scale
    mat_im = sign * interior_part * symbol_profile * jnp.sin(turn) / scale
    return (mat_re, mat_im)

def disperse(ext, mat_re, mat_im, reach):
    pols, parts, chans, segment_length = ext.shape
    blocks = segment_length // reach - 2
    rows = ext.reshape(pols, parts, chans, blocks + 2, reach)
    window = jnp.concatenate([rows[:, :, :, 0:blocks], rows[:, :, :, 1:blocks + 1], rows[:, :, :, 2:blocks + 2]], axis=4)
    real = window[:, 0]
    imag = window[:, 1]
    high = lax.Precision.HIGHEST
    out_re = jnp.einsum('pcjq,cqn->pcjn', real, mat_re, precision=high) - jnp.einsum('pcjq,cqn->pcjn', imag, mat_im, precision=high)
    out_im = jnp.einsum('pcjq,cqn->pcjn', real, mat_im, precision=high) + jnp.einsum('pcjq,cqn->pcjn', imag, mat_re, precision=high)
    return jnp.stack([out_re, out_im], axis=1).reshape(pols, parts, chans, blocks * reach)

def rotate(ext, sign, own, total):
    angle = sign * GAMMA * (2.0 * total[None, :] - own)
    cosine = jnp.cos(angle)
    sine = jnp.sin(angle)
    real = ext[:, 0]
    imag = ext[:, 1]
    return jnp.stack([real * cosine - imag * sine, real * sine + imag * cosine], axis=1)

def periodic_filter(current, tables):
    ext = jnp.concatenate([current[..., -FILTER_HALF_TAPS:], current, current[..., :FILTER_HALF_TAPS]], axis=3)

    def single(args):
        piece, m_re, m_im = args
        return disperse(piece[:, :, None], m_re[None], m_im[None], FILTER_HALF_TAPS)[:, :, 0]
    out = lax.map(single, (jnp.moveaxis(ext, 2, 0), tables[0], tables[1]))
    return jnp.moveaxis(out, 0, 2)

def nonlinear(current, sign):
    own = lax.optimization_barrier(jnp.sum(jnp.square(current), axis=(0, 1)))
    total = lax.optimization_barrier(jnp.sum(own, axis=0))
    return rotate(current, sign, own, total)

def slot_power(current):
    return lax.optimization_barrier(jnp.sum(jnp.square(current), axis=(0, 1, 3))) / TIME_SAMPLES

def reference(field, noise, assign):
    forward = tap_tables(assign, 1.0, FILTER_HALF_TAPS, OPTICAL_CHANNELS)
    backward = tap_tables(assign, -1.0, FILTER_HALF_TAPS, OPTICAL_CHANNELS)
    current = field
    for span in range(FIBER_SECTIONS):
        for step in range(STEPS):
            current = periodic_filter(current, forward) * ATT
            current = nonlinear(current, 1.0)
        gain = lax.rsqrt(slot_power(current) + EPS)
        current = current * gain[None, None, :, None] + noise[span]
    received = current
    for span in range(FIBER_SECTIONS):
        rescale = jnp.sqrt(ATT ** (2 * STEPS) / (slot_power(current) + EPS))
        current = current * rescale[None, None, :, None]
        for step in range(STEPS):
            current = nonlinear(current, -1.0) / ATT
            current = periodic_filter(current, backward)
    return (received, current)
```

```python
import functools
import jax
import jax.numpy as jnp
from jax import lax
from jax.experimental import pallas as pl
from jax.experimental.pallas import tpu as pltpu
from jax.sharding import PartitionSpec as P

OPTICAL_CHANNELS = 64
REACH = 128
STEPS = 2
ATT = 0.955
GAMMA = 0.004
WALK = 0.5
SPREAD = 0.4
CHIRP = 0.25
EPS = 1e-06
GROUP = 8
MESH = pl.DeviceIdType.MESH


def tap_rows(channel_ids):
    lag = jnp.arange(-REACH, 2 * REACH, dtype=jnp.int32)
    centre = (
        WALK * REACH * (2.0 * channel_ids.astype(jnp.float32) - (OPTICAL_CHANNELS - 1))
        / (OPTICAL_CHANNELS - 1)
    )[:, None]
    width = SPREAD * REACH
    taps = jnp.arange(-REACH, REACH + 1, dtype=jnp.int32).astype(jnp.float32)
    scale = jnp.sqrt(
        jnp.sum(jnp.exp(-2.0 * jnp.square((taps[None, :] - centre) / width)), axis=1)
    )[:, None]
    rows, ends = [], []
    for sign, factor in ((1.0, ATT), (-1.0, 1.0 / ATT)):
        offset = sign * lag.astype(jnp.float32)[None] - centre
        profile = factor * jnp.exp(-jnp.square(offset / width)) / scale
        turn = jnp.square(offset) / (2.0 * CHIRP * REACH)
        for part in (profile * jnp.cos(turn), sign * profile * jnp.sin(turn)):
            rows += [part[:, :REACH], part[:, REACH : 2 * REACH]]
            ends.append(jnp.broadcast_to(part[:, 2 * REACH : 2 * REACH + 1], part[:, :REACH].shape))
    rows += ends
    rows += [jnp.zeros_like(rows[0])] * 4
    return jnp.stack(rows, axis=1)


def cos_sin(angle):
    n = jnp.floor(angle * 0.3183098861837907 + 0.5)
    r = ((angle - n * 3.140625) - n * 9.67502593994140625e-4) - n * 1.509957990978376432e-7
    sgn = 1.0 - 2.0 * (n - 2.0 * jnp.floor(0.5 * n))
    z = r * r
    s = -1.0 / 39916800.0
    for k in (1.0 / 362880.0, -1.0 / 5040.0, 1.0 / 120.0, -1.0 / 6.0, 1.0):
        s = s * z + k
    c = 1.0 / 479001600.0
    for k in (-1.0 / 3628800.0, 1.0 / 40320.0, -1.0 / 720.0, 1.0 / 24.0, -0.5, 1.0):
        c = c * z + k
    return c * sgn, s * (r * sgn)


def kernel(
    nt, nc, total_len,
    field_hbm, noise_hbm, x_ref, noise_ref, taps_ref,
    rec_ref, out_ref,
    t_hi, t_lo, y_ref, z_ref, pw_ref, h_ref, e_ref, hr_ref, tsend, trecv, tot_ref, stat, ssend, srecv, gain_ref,
    h_send, h_recv, e_send, e_recv, c_send, c_recv, s_send, s_recv,
):
    slots = x_ref.shape[0]
    length = field_hbm.shape[3]
    groups = slots // GROUP
    tm, ch = lax.axis_index("tm"), lax.axis_index("chan")
    right, left = lax.rem(tm + 1, nt), lax.rem(tm + nt - 1, nt)
    row = lax.broadcasted_iota(jnp.int32, (8, 128), 0)

    barrier = pltpu.get_barrier_semaphore()

    def greet(d, _):
        pl.semaphore_signal(
            barrier, inc=1, device_id={"tm": lax.rem(tm + d, nt)}, device_id_type=MESH
        )
        return 0

    lax.fori_loop(1, nt, greet, 0)
    for d in range(1, nc):
        pl.semaphore_signal(
            barrier, inc=1, device_id={"chan": lax.rem(ch + d, nc)}, device_id_type=MESH
        )
    pl.semaphore_wait(barrier, nt - 1 + nc - 1)

    def first_edge(k, side):
        source = (field_hbm, noise_hbm)[k]
        start = length - REACH if side == 0 else 0
        return pltpu.make_async_remote_copy(
            src_ref=source.at[:, :, :, pl.ds(start, REACH)],
            dst_ref=h_ref.at[k, side],
            send_sem=h_send.at[k, side],
            recv_sem=h_recv.at[k, side],
            device_id={"tm": right if side == 0 else left},
            device_id_type=MESH,
        )

    for k in range(2):
        for side in range(2):
            first_edge(k, side).start()

    def edge(step, side, g):
        where = (slice(None), slice(None), pl.ds(g * GROUP, GROUP), slice(None))
        return pltpu.make_async_remote_copy(
            src_ref=e_ref.at[(step, side) + where],
            dst_ref=h_ref.at[(2 + step, side) + where],
            send_sem=e_send.at[step, side, g],
            recv_sem=e_recv.at[step, side, g],
            device_id={"tm": right if side == 0 else left},
            device_id_type=MESH,
        )

    q = lax.broadcasted_iota(jnp.int32, (128, 128), 0)
    n = lax.broadcasted_iota(jnp.int32, (128, 128), 1)
    upper, diag = n >= q, n == q

    def build(sgn, lo, hi):
        def body(c, _):
            for part in range(2):
                def spread(i):
                    v = jnp.broadcast_to(taps_ref[c, pl.ds(i, 1), :], (128, 128))
                    return pltpu.roll(v, 0, 1, stride=1, stride_axis=0)

                neg = spread(sgn * 4 + part * 2)
                pos = spread(sgn * 4 + part * 2 + 1)
                last = taps_ref[c, pl.ds(8 + sgn * 2 + part, 1), :]
                blocks = (
                    jnp.where(upper, jnp.where(diag, last, 0.0), pos),
                    jnp.where(upper, pos, neg),
                    jnp.where(upper, neg, 0.0),
                )
                for b, t in enumerate(blocks):
                    big = t.astype(jnp.bfloat16)
                    small = (t - big.astype(jnp.float32)).astype(jnp.bfloat16)
                    t_hi[sgn, c, pl.ds(b * 128, 128), pl.ds(part * 128, 128)] = big
                    t_lo[sgn, c, pl.ds(b * 128, 128), pl.ds(part * 128, 128)] = small
            return 0

        lax.fori_loop(lo, hi, body, 0)

    def filtered(sgn, c, xs, halo):
        wide = []
        for part in range(2):
            for pol in range(2):
                v = xs[part * 2 + pol]
                before = halo[0, pol, part, pl.ds(c, 1), :]
                after = halo[1, pol, part, pl.ds(c, 1), :]
                wide.append(
                    jnp.concatenate(
                        [
                            jnp.where(row == 0, before, pltpu.roll(v, 1, 0)),
                            v,
                            jnp.where(row == 7, after, pltpu.roll(v, 7, 0)),
                        ],
                        axis=1,
                    )
                )
        win = jnp.concatenate(wide, axis=0)
        big = win.astype(jnp.bfloat16)
        small = (win - big.astype(jnp.float32)).astype(jnp.bfloat16)
        a = jnp.dot(
            jnp.concatenate([big, small], axis=0), t_hi[sgn, c], preferred_element_type=jnp.float32
        )
        b = jnp.dot(big, t_lo[sgn, c], preferred_element_type=jnp.float32)
        s = a[:32] + a[32:] + b
        re = s[:16, :128] - s[16:, 128:]
        im = s[:16, 128:] + s[16:, :128]
        return (re[:8], re[8:], im[:8], im[8:])

    def load(ref, c):
        return [ref[c, pl.ds(8 * i, 8), :] for i in range(4)]

    def store(ref, c, vs):
        for i in range(4):
            ref[c, pl.ds(8 * i, 8), :] = vs[i]

    def power(vs):
        return (vs[0] * vs[0] + vs[1] * vs[1]) + (vs[2] * vs[2] + vs[3] * vs[3])

    def turned(sign, vs, own, total):
        co, si = cos_sin((sign * GAMMA) * (2.0 * total - own))
        a, b, d, e = vs
        return (a * co - d * si, b * co - e * si, a * si + d * co, b * si + e * co)

    def run_filter(sgn, get, halo, step):
        total = jnp.zeros((8, 128), jnp.float32)
        for g in range(groups):
            def body(c, total):
                ys = filtered(sgn, c, get(c), halo)
                if step is None:
                    store(out_ref, c, ys)
                    return total
                own = power(ys)
                store(y_ref, c, ys)
                pw_ref[c] = own
                for part in range(2):
                    for pol in range(2):
                        v = ys[part * 2 + pol]
                        e_ref[step, 0, pol, part, pl.ds(c, 1), :] = v[7:8]
                        e_ref[step, 1, pol, part, pl.ds(c, 1), :] = v[0:1]
                return total + own

            total = lax.fori_loop(g * GROUP, (g + 1) * GROUP, body, total, unroll=4)
            if step is not None:
                edge(step, 0, g).start()
                edge(step, 1, g).start()
        return total

    def edges_arrived(step):
        for g in range(groups):
            for side in range(2):
                edge(step, side, g).wait()

    def chan_copy(k, d):
        return pltpu.make_async_remote_copy(
            src_ref=tsend.at[k],
            dst_ref=trecv.at[k, d - 1],
            send_sem=c_send.at[k, d - 1],
            recv_sem=c_recv.at[k, d - 1],
            device_id={"chan": lax.rem(ch + d, nc)},
            device_id_type=MESH,
        )

    def side_power(ref, side):
        out = None
        for pol in range(2):
            for part in range(2):
                v = ref[side, pol, part]
                out = v * v if out is None else out + v * v
        return out

    def exchange_total(k, total, halo, beside):
        tsend[k, pl.ds(0, 8), :] = total
        before = jnp.sum(side_power(halo, 0), axis=0, keepdims=True)
        after = jnp.sum(side_power(halo, 1), axis=0, keepdims=True)
        tsend[k, pl.ds(8, 8), :] = jnp.where(
            row == 0, before, jnp.where(row == 1, after, 0.0)
        )
        for d in range(1, nc):
            chan_copy(k, d).start()
        beside()
        whole = tsend[k]
        for d in range(1, nc):
            chan_copy(k, d).wait()
            whole = whole + trecv[k, d - 1]
        tot_ref[...] = whole

    def turn_halo(sign, halo):
        for side in range(2):
            own = side_power(halo, side)
            co, si = cos_sin(
                (sign * GAMMA) * (2.0 * tot_ref[pl.ds(8 + side, 1), :] - own)
            )
            for pol in range(2):
                a, b = halo[side, pol, 0], halo[side, pol, 1]
                hr_ref[side, pol, 0] = a * co - b * si
                hr_ref[side, pol, 1] = a * si + b * co

    build(0, 0, slots)
    for side in range(2):
        first_edge(0, side).wait()
    total = run_filter(0, lambda c: load(x_ref, c), h_ref.at[0], 0)

    edges_arrived(0)
    half = slots // 2
    exchange_total(0, total, h_ref.at[2], lambda: build(1, 0, half))
    turn_halo(1.0, h_ref.at[2])

    def forward_rotated(c):
        return turned(1.0, load(y_ref, c), pw_ref[c], tot_ref[pl.ds(0, 8), :])

    total = run_filter(0, forward_rotated, hr_ref, 1)
    edges_arrived(1)
    three = half + slots // 4
    exchange_total(1, total, h_ref.at[3], lambda: build(1, half, three))

    def sums(c, _):
        vs = forward_rotated(c)
        ns = load(noise_ref, c)
        store(z_ref, c, vs)
        cross = (vs[0] * ns[0] + vs[1] * ns[1]) + (vs[2] * ns[2] + vs[3] * ns[3])
        for i, v in enumerate((pw_ref[c], cross, power(ns))):
            stat[i, pl.ds(c, 1), :] = jnp.sum(v, axis=0, keepdims=True)
        return 0

    lax.fori_loop(0, slots, sums, 0, unroll=4)
    own_lane = lax.broadcasted_iota(jnp.int32, (slots, 128), 1) == lax.broadcasted_iota(
        jnp.int32, (slots, 128), 0
    )
    packed = jnp.zeros((8, 128), jnp.float32)
    for i in range(3):
        col = jnp.sum(stat[i], axis=1, keepdims=True)
        line = jnp.sum(jnp.where(own_lane, col, 0.0), axis=0, keepdims=True)
        packed = jnp.where(row == i, line, packed)
    ssend[...] = packed

    def stat_copy(d):
        return pltpu.make_async_remote_copy(
            src_ref=ssend,
            dst_ref=srecv.at[d - 1],
            send_sem=s_send.at[d - 1],
            recv_sem=s_recv.at[d - 1],
            device_id={"tm": lax.rem(tm + d, nt)},
            device_id_type=MESH,
        )

    def stat_start(d, _):
        stat_copy(d).start()
        return 0

    lax.fori_loop(1, nt, stat_start, 0)
    build(1, three, slots)
    turn_halo(1.0, h_ref.at[3])
    for side in range(2):
        first_edge(1, side).wait()

    def stat_add(d, acc):
        stat_copy(d).wait()
        return acc + srecv[d - 1]

    sums_all = lax.fori_loop(1, nt, stat_add, packed)
    field_sq, cross, noise_sq = sums_all[0:1], sums_all[1:2], sums_all[2:3]
    gain = lax.rsqrt(field_sq / total_len + EPS)
    arrival = (gain * gain * field_sq + 2.0 * gain * cross + noise_sq) / total_len
    rescale = jnp.sqrt(ATT ** (2 * STEPS) / (arrival + EPS))
    for i, v in enumerate((gain, rescale)):
        col = jnp.sum(jnp.where(own_lane, v, 0.0), axis=1, keepdims=True)
        gain_ref[i] = jnp.broadcast_to(col, (slots, 128))

    def amplify(c, total):
        g = gain_ref[0, pl.ds(c, 1), :]
        r = gain_ref[1, pl.ds(c, 1), :]
        vs, ns = load(z_ref, c), load(noise_ref, c)
        rec = [v * g + m for v, m in zip(vs, ns)]
        store(rec_ref, c, rec)
        back = [v * r for v in rec]
        store(y_ref, c, back)
        own = power(back)
        pw_ref[c] = own
        return total + own

    total = lax.fori_loop(0, slots, amplify, jnp.zeros((8, 128), jnp.float32), unroll=4)
    for side in range(2):
        for pol in range(2):
            for part in range(2):
                hr_ref[side, pol, part] = (
                    hr_ref[side, pol, part] * gain_ref[0] + h_ref[1, side, pol, part]
                ) * gain_ref[1]
    exchange_total(2, total, hr_ref, lambda: None)
    turn_halo(-1.0, hr_ref)

    def backward_rotated(c):
        return turned(-1.0, load(y_ref, c), pw_ref[c], tot_ref[pl.ds(0, 8), :])

    total = run_filter(1, backward_rotated, hr_ref, 2)
    edges_arrived(2)
    exchange_total(3, total, h_ref.at[4], lambda: None)
    turn_halo(-1.0, h_ref.at[4])
    run_filter(1, backward_rotated, hr_ref, None)


def on_device(field, noise, assign):
    nt, nc = lax.axis_size("tm"), lax.axis_size("chan")
    noise = noise[0]
    slots, length = field.shape[2], field.shape[3]
    blocks = length // REACH

    def arranged(a):
        a = a.reshape(2, 2, slots, blocks, REACH)
        return a.transpose(2, 1, 0, 3, 4).reshape(slots, 4 * blocks, REACH)

    def restored(a):
        a = a.reshape(slots, 2, 2, blocks, REACH)
        return a.transpose(2, 1, 0, 3, 4).reshape(2, 2, slots, length)

    f32, bf16 = jnp.float32, jnp.bfloat16
    vmem = pl.BlockSpec(memory_space=pltpu.VMEM)
    hbm = pl.BlockSpec(memory_space=pl.ANY)
    shape = jax.ShapeDtypeStruct((slots, 4 * blocks, REACH), f32)
    dma = pltpu.SemaphoreType.DMA
    received, recovered = pl.pallas_call(
        functools.partial(kernel, nt, nc, float(nt * length)),
        out_shape=(shape, shape),
        in_specs=[hbm, hbm, vmem, vmem, vmem],
        out_specs=(vmem, vmem),
        scratch_shapes=[
            pltpu.VMEM((2, slots, 3 * REACH, 2 * REACH), bf16),
            pltpu.VMEM((2, slots, 3 * REACH, 2 * REACH), bf16),
            pltpu.VMEM((slots, 4 * blocks, REACH), f32),
            pltpu.VMEM((slots, 4 * blocks, REACH), f32),
            pltpu.VMEM((slots, blocks, REACH), f32),
            pltpu.VMEM((5, 2, 2, 2, slots, REACH), f32),
            pltpu.VMEM((3, 2, 2, 2, slots, REACH), f32),
            pltpu.VMEM((2, 2, 2, slots, REACH), f32),
            pltpu.VMEM((4, 16, REACH), f32),
            pltpu.VMEM((4, nc - 1, 16, REACH), f32),
            pltpu.VMEM((16, REACH), f32),
            pltpu.VMEM((3, slots, REACH), f32),
            pltpu.VMEM((8, REACH), f32),
            pltpu.VMEM((nt - 1, 8, REACH), f32),
            pltpu.VMEM((2, slots, REACH), f32),
            dma((2, 2)),
            dma((2, 2)),
            dma((3, 2, slots // GROUP)),
            dma((3, 2, slots // GROUP)),
            dma((4, nc - 1)),
            dma((4, nc - 1)),
            dma((nt - 1,)),
            dma((nt - 1,)),
        ],
        compiler_params=pltpu.CompilerParams(
            collective_id=0, has_side_effects=True, vmem_limit_bytes=48 * 1024 * 1024
        ),
    )(field, noise, arranged(field), arranged(noise), tap_rows(assign))
    return restored(received), restored(recovered)


def solution(mesh):
    placed = (P(None, None, "chan", "tm"), P(None, None, None, "chan", "tm"), P("chan"))
    return jax.shard_map(
        on_device,
        mesh=mesh,
        in_specs=placed,
        out_specs=(P(None, None, "chan", "tm"), P(None, None, "chan", "tm")),
        check_vma=False,
    )
```

```python
import functools
import jax
import jax.numpy as jnp
from jax import lax
from jax.experimental import pallas as pl
from jax.experimental.pallas import tpu as pltpu
from jax.sharding import PartitionSpec as P

OPTICAL_CHANNELS = 64
REACH = 128
STEPS = 2
ATT = 0.955
GAMMA = 0.004
WALK = 0.5
SPREAD = 0.4
CHIRP = 0.25
EPS = 1e-06
GROUP = 8
MESH = pl.DeviceIdType.MESH


def tap_rows(channel_ids):
    lag = jnp.arange(-REACH, 2 * REACH, dtype=jnp.int32)
    centre = (
        WALK * REACH * (2.0 * channel_ids.astype(jnp.float32) - (OPTICAL_CHANNELS - 1))
        / (OPTICAL_CHANNELS - 1)
    )[:, None]
    width = SPREAD * REACH
    taps = jnp.arange(-REACH, REACH + 1, dtype=jnp.int32).astype(jnp.float32)
    scale = jnp.sqrt(
        jnp.sum(jnp.exp(-2.0 * jnp.square((taps[None, :] - centre) / width)), axis=1)
    )[:, None]
    rows, ends = [], []
    for sign, factor in ((1.0, ATT), (-1.0, 1.0 / ATT)):
        offset = sign * lag.astype(jnp.float32)[None] - centre
        profile = factor * jnp.exp(-jnp.square(offset / width)) / scale
        turn = jnp.square(offset) / (2.0 * CHIRP * REACH)
        for part in (profile * jnp.cos(turn), sign * profile * jnp.sin(turn)):
            rows += [part[:, :REACH], part[:, REACH : 2 * REACH]]
            ends.append(jnp.broadcast_to(part[:, 2 * REACH : 2 * REACH + 1], part[:, :REACH].shape))
    rows += ends
    rows += [jnp.zeros_like(rows[0])] * 4
    return jnp.stack(rows, axis=1)


def cos_sin(angle):
    n = jnp.floor(angle * 0.3183098861837907 + 0.5)
    r = ((angle - n * 3.140625) - n * 9.67502593994140625e-4) - n * 1.509957990978376432e-7
    sgn = 1.0 - 2.0 * (n - 2.0 * jnp.floor(0.5 * n))
    z = r * r
    s = -1.0 / 39916800.0
    for k in (1.0 / 362880.0, -1.0 / 5040.0, 1.0 / 120.0, -1.0 / 6.0, 1.0):
        s = s * z + k
    c = 1.0 / 479001600.0
    for k in (-1.0 / 3628800.0, 1.0 / 40320.0, -1.0 / 720.0, 1.0 / 24.0, -0.5, 1.0):
        c = c * z + k
    return c * sgn, s * (r * sgn)


def kernel(
    nt, nc, total_len,
    field_hbm, noise_hbm, x_ref, noise_ref, taps_ref,
    rec_ref, out_ref,
    lhs_ref, t_hi, t_lo, y_ref, z_ref, pw_ref, h_ref, e_ref, hr_ref, tsend, trecv, tot_ref, stat, ssend, srecv, gain_ref,
    h_send, h_recv, e_send, e_recv, c_send, c_recv, s_send, s_recv,
):
    slots = x_ref.shape[0]
    length = field_hbm.shape[3]
    groups = slots // GROUP
    tm, ch = lax.axis_index("tm"), lax.axis_index("chan")
    right, left = lax.rem(tm + 1, nt), lax.rem(tm + nt - 1, nt)
    row = lax.broadcasted_iota(jnp.int32, (8, 128), 0)

    barrier = pltpu.get_barrier_semaphore()

    def greet(d, _):
        pl.semaphore_signal(
            barrier, inc=1, device_id={"tm": lax.rem(tm + d, nt)}, device_id_type=MESH
        )
        return 0

    lax.fori_loop(1, nt, greet, 0)
    for d in range(1, nc):
        pl.semaphore_signal(
            barrier, inc=1, device_id={"chan": lax.rem(ch + d, nc)}, device_id_type=MESH
        )
    pl.semaphore_wait(barrier, nt - 1 + nc - 1)

    def first_edge(k, side):
        source = (field_hbm, noise_hbm)[k]
        start = length - REACH if side == 0 else 0
        return pltpu.make_async_remote_copy(
            src_ref=source.at[:, :, :, pl.ds(start, REACH)],
            dst_ref=h_ref.at[k, side],
            send_sem=h_send.at[k, side],
            recv_sem=h_recv.at[k, side],
            device_id={"tm": right if side == 0 else left},
            device_id_type=MESH,
        )

    for k in range(2):
        for side in range(2):
            first_edge(k, side).start()

    def edge(step, side, g):
        where = (slice(None), slice(None), pl.ds(g * GROUP, GROUP), slice(None))
        return pltpu.make_async_remote_copy(
            src_ref=e_ref.at[(step, side) + where],
            dst_ref=h_ref.at[(2 + step, side) + where],
            send_sem=e_send.at[step, side, g],
            recv_sem=e_recv.at[step, side, g],
            device_id={"tm": right if side == 0 else left},
            device_id_type=MESH,
        )

    q = lax.broadcasted_iota(jnp.int32, (128, 128), 0)
    n = lax.broadcasted_iota(jnp.int32, (128, 128), 1)
    upper, diag = n >= q, n == q

    def build(sgn, lo, hi):
        def body(c, _):
            for part in range(2):
                def spread(i):
                    v = jnp.broadcast_to(taps_ref[c, pl.ds(i, 1), :], (128, 128))
                    return pltpu.roll(v, 0, 1, stride=1, stride_axis=0)

                neg = spread(sgn * 4 + part * 2)
                pos = spread(sgn * 4 + part * 2 + 1)
                last = taps_ref[c, pl.ds(8 + sgn * 2 + part, 1), :]
                blocks = (
                    jnp.where(upper, jnp.where(diag, last, 0.0), pos),
                    jnp.where(upper, pos, neg),
                    jnp.where(upper, neg, 0.0),
                )
                for b, t in enumerate(blocks):
                    big = t.astype(jnp.bfloat16)
                    small = (t - big.astype(jnp.float32)).astype(jnp.bfloat16)
                    t_hi[sgn, c, pl.ds(b * 128, 128), pl.ds(part * 128, 128)] = big
                    t_lo[sgn, c, pl.ds(b * 128, 128), pl.ds(part * 128, 128)] = small
            return 0

        lax.fori_loop(lo, hi, body, 0, unroll=2)

    def load(ref, c0):
        return [ref[pl.ds(c0, GROUP), pl.ds(8 * i, 8), :] for i in range(4)]

    def store(ref, c0, vs):
        for i in range(4):
            ref[pl.ds(c0, GROUP), pl.ds(8 * i, 8), :] = vs[i]

    def power(vs):
        return (vs[0] * vs[0] + vs[1] * vs[1]) + (vs[2] * vs[2] + vs[3] * vs[3])

    def turned(sign, vs, own, total):
        co, si = cos_sin((sign * GAMMA) * (2.0 * total - own))
        a, b, d, e = vs
        return (a * co - d * si, b * co - e * si, a * si + d * co, b * si + e * co)

    row3 = lax.broadcasted_iota(jnp.int32, (GROUP, 8, 128), 1)

    def windows(buf, c0, xs, halo):
        def spread(side, pol, part):
            return jnp.stack(
                [
                    jnp.broadcast_to(halo[side, pol, part, pl.ds(c0 + i, 1), :], (8, 128))
                    for i in range(GROUP)
                ]
            )

        for part in range(2):
            cuts = ([], [], [])
            for pol in range(2):
                v = xs[part * 2 + pol]
                cuts[0].append(jnp.where(row3 == 0, spread(0, pol, part), pltpu.roll(v, 1, 1)))
                cuts[1].append(v)
                cuts[2].append(jnp.where(row3 == 7, spread(1, pol, part), pltpu.roll(v, 7, 1)))
            for k in range(3):
                win = jnp.concatenate(cuts[k], axis=1)
                big = win.astype(jnp.bfloat16)
                small = (win - big.astype(jnp.float32)).astype(jnp.bfloat16)
                lhs_ref[buf, :, pl.ds(part * 16, 16), pl.ds(k * 128, 128)] = big
                lhs_ref[buf, :, pl.ds(32 + part * 16, 16), pl.ds(k * 128, 128)] = small

    def run_filter(sgn, get, halo, step):
        total = jnp.zeros((8, 128), jnp.float32)
        windows(0, 0, get(0), halo)
        for g in range(groups):
            if g + 1 < groups:
                windows((g + 1) % 2, (g + 1) * GROUP, get((g + 1) * GROUP), halo)
            for i in range(GROUP):
                c = g * GROUP + i
                lhs = lhs_ref[g % 2, i]
                a = jnp.dot(lhs, t_hi[sgn, c], preferred_element_type=jnp.float32)
                b = jnp.dot(lhs[:32], t_lo[sgn, c], preferred_element_type=jnp.float32)
                s = a[:32] + a[32:] + b
                re = s[:16, :128] - s[16:, 128:]
                im = s[:16, 128:] + s[16:, :128]
                if step is None:
                    out_ref[c, pl.ds(0, 16), :] = re
                    out_ref[c, pl.ds(16, 16), :] = im
                    continue
                ys = (re[:8], re[8:], im[:8], im[8:])
                own = power(ys)
                total = total + own
                y_ref[c, pl.ds(0, 16), :] = re
                y_ref[c, pl.ds(16, 16), :] = im
                pw_ref[c] = own
                for part in range(2):
                    for pol in range(2):
                        v = ys[part * 2 + pol]
                        e_ref[step, 0, pol, part, pl.ds(c, 1), :] = v[7:8]
                        e_ref[step, 1, pol, part, pl.ds(c, 1), :] = v[0:1]
            if step is not None:
                edge(step, 0, g).start()
                edge(step, 1, g).start()
        return total

    def edges_arrived(step):
        for g in range(groups):
            for side in range(2):
                edge(step, side, g).wait()

    def chan_copy(k, d):
        return pltpu.make_async_remote_copy(
            src_ref=tsend.at[k],
            dst_ref=trecv.at[k, d - 1],
            send_sem=c_send.at[k, d - 1],
            recv_sem=c_recv.at[k, d - 1],
            device_id={"chan": lax.rem(ch + d, nc)},
            device_id_type=MESH,
        )

    def side_power(ref, side):
        out = None
        for pol in range(2):
            for part in range(2):
                v = ref[side, pol, part]
                out = v * v if out is None else out + v * v
        return out

    def exchange_start(k, value):
        tsend[k] = value
        for d in range(1, nc):
            chan_copy(k, d).start()

    def exchange_end(k):
        whole = tsend[k]
        for d in range(1, nc):
            chan_copy(k, d).wait()
            whole = whole + trecv[k, d - 1]
        tot_ref[pl.ds(8 * (k // 4), 8), :] = whole

    def halo_total(halo):
        before = jnp.sum(side_power(halo, 0), axis=0, keepdims=True)
        after = jnp.sum(side_power(halo, 1), axis=0, keepdims=True)
        return jnp.where(row == 0, before, jnp.where(row == 1, after, 0.0))

    def halo_exchange(step, k):
        edges_arrived(step)
        exchange_start(4 + k, halo_total(h_ref.at[2 + step]))
        exchange_end(4 + k)

    def turn_all(rotated):
        def body(g, _):
            c0 = pl.multiple_of(g * GROUP, GROUP)
            store(y_ref, c0, rotated(c0))
            return 0

        lax.fori_loop(0, groups, body, 0)

    def kept(c0):
        return load(y_ref, c0)

    def turn_halo(sign, halo):
        for side in range(2):
            own = side_power(halo, side)
            co, si = cos_sin(
                (sign * GAMMA) * (2.0 * tot_ref[pl.ds(8 + side, 1), :] - own)
            )
            for pol in range(2):
                a, b = halo[side, pol, 0], halo[side, pol, 1]
                hr_ref[side, pol, 0] = a * co - b * si
                hr_ref[side, pol, 1] = a * si + b * co

    build(0, 0, slots)
    for side in range(2):
        first_edge(0, side).wait()
    total = run_filter(0, lambda c: load(x_ref, c), h_ref.at[0], 0)

    half = slots // 2
    exchange_start(0, total)
    build(1, 0, half)
    exchange_end(0)

    def forward_rotated(c):
        own = pw_ref[pl.ds(c, GROUP)]
        return turned(1.0, load(y_ref, c), own, tot_ref[pl.ds(0, 8), :][None])

    turn_all(forward_rotated)
    halo_exchange(0, 0)
    turn_halo(1.0, h_ref.at[2])

    total = run_filter(0, kept, hr_ref, 1)
    exchange_start(1, total)
    exchange_end(1)

    def sums(g, _):
        c0 = pl.multiple_of(g * GROUP, GROUP)
        vs = forward_rotated(c0)
        ns = load(noise_ref, c0)
        store(z_ref, c0, vs)
        cross = (vs[0] * ns[0] + vs[1] * ns[1]) + (vs[2] * ns[2] + vs[3] * ns[3])
        for i, v in enumerate((pw_ref[pl.ds(c0, GROUP)], cross, power(ns))):
            stat[i, pl.ds(c0, GROUP), :] = jnp.sum(v, axis=1)
        return 0

    lax.fori_loop(0, groups, sums, 0)
    own_lane = lax.broadcasted_iota(jnp.int32, (slots, 128), 1) == lax.broadcasted_iota(
        jnp.int32, (slots, 128), 0
    )
    packed = jnp.zeros((8, 128), jnp.float32)
    for i in range(3):
        col = jnp.sum(stat[i], axis=1, keepdims=True)
        line = jnp.sum(jnp.where(own_lane, col, 0.0), axis=0, keepdims=True)
        packed = jnp.where(row == i, line, packed)
    ssend[...] = packed

    def stat_copy(d):
        return pltpu.make_async_remote_copy(
            src_ref=ssend,
            dst_ref=srecv.at[d - 1],
            send_sem=s_send.at[d - 1],
            recv_sem=s_recv.at[d - 1],
            device_id={"tm": lax.rem(tm + d, nt)},
            device_id_type=MESH,
        )

    def stat_start(d, _):
        stat_copy(d).start()
        return 0

    lax.fori_loop(1, nt, stat_start, 0)
    build(1, half, slots)
    halo_exchange(1, 1)
    turn_halo(1.0, h_ref.at[3])
    for side in range(2):
        first_edge(1, side).wait()

    def stat_add(d, acc):
        stat_copy(d).wait()
        return acc + srecv[d - 1]

    sums_all = lax.fori_loop(1, nt, stat_add, packed)
    field_sq, cross, noise_sq = sums_all[0:1], sums_all[1:2], sums_all[2:3]
    gain = lax.rsqrt(field_sq / total_len + EPS)
    arrival = (gain * gain * field_sq + 2.0 * gain * cross + noise_sq) / total_len
    rescale = jnp.sqrt(ATT ** (2 * STEPS) / (arrival + EPS))
    for i, v in enumerate((gain, rescale)):
        col = jnp.sum(jnp.where(own_lane, v, 0.0), axis=1, keepdims=True)
        gain_ref[i] = jnp.broadcast_to(col, (slots, 128))

    def amplify(k, total):
        c0 = pl.multiple_of(k * GROUP, GROUP)

        def spread(i):
            return jnp.stack(
                [
                    jnp.broadcast_to(gain_ref[i, pl.ds(c0 + j, 1), :], (8, 128))
                    for j in range(GROUP)
                ]
            )

        g, r = spread(0), spread(1)
        vs, ns = load(z_ref, c0), load(noise_ref, c0)
        rec = [v * g + m for v, m in zip(vs, ns)]
        store(rec_ref, c0, rec)
        back = [v * r for v in rec]
        store(y_ref, c0, back)
        own = power(back)
        pw_ref[pl.ds(c0, GROUP)] = own
        return total + jnp.sum(own, axis=0)

    total = lax.fori_loop(0, groups, amplify, jnp.zeros((8, 128), jnp.float32))
    for side in range(2):
        for pol in range(2):
            for part in range(2):
                hr_ref[side, pol, part] = (
                    hr_ref[side, pol, part] * gain_ref[0] + h_ref[1, side, pol, part]
                ) * gain_ref[1]
    exchange_start(2, total)
    exchange_start(6, halo_total(hr_ref))
    exchange_end(2)
    exchange_end(6)
    turn_halo(-1.0, hr_ref)

    def backward_rotated(c):
        own = pw_ref[pl.ds(c, GROUP)]
        return turned(-1.0, load(y_ref, c), own, tot_ref[pl.ds(0, 8), :][None])

    total = run_filter(1, backward_rotated, hr_ref, 2)
    exchange_start(3, total)
    exchange_end(3)
    turn_all(backward_rotated)
    halo_exchange(2, 3)
    turn_halo(-1.0, h_ref.at[4])
    run_filter(1, kept, hr_ref, None)


def on_device(field, noise, assign):
    nt, nc = lax.axis_size("tm"), lax.axis_size("chan")
    noise = noise[0]
    slots, length = field.shape[2], field.shape[3]
    blocks = length // REACH

    def arranged(a):
        a = a.reshape(2, 2, slots, blocks, REACH)
        return a.transpose(2, 1, 0, 3, 4).reshape(slots, 4 * blocks, REACH)

    def restored(a):
        a = a.reshape(slots, 2, 2, blocks, REACH)
        return a.transpose(2, 1, 0, 3, 4).reshape(2, 2, slots, length)

    f32, bf16 = jnp.float32, jnp.bfloat16
    vmem = pl.BlockSpec(memory_space=pltpu.VMEM)
    hbm = pl.BlockSpec(memory_space=pl.ANY)
    shape = jax.ShapeDtypeStruct((slots, 4 * blocks, REACH), f32)
    dma = pltpu.SemaphoreType.DMA
    received, recovered = pl.pallas_call(
        functools.partial(kernel, nt, nc, float(nt * length)),
        out_shape=(shape, shape),
        in_specs=[hbm, hbm, vmem, vmem, vmem],
        out_specs=(vmem, vmem),
        scratch_shapes=[
            pltpu.VMEM((2, GROUP, 64, 3 * REACH), bf16),
            pltpu.VMEM((2, slots, 3 * REACH, 2 * REACH), bf16),
            pltpu.VMEM((2, slots, 3 * REACH, 2 * REACH), bf16),
            pltpu.VMEM((slots, 4 * blocks, REACH), f32),
            pltpu.VMEM((slots, 4 * blocks, REACH), f32),
            pltpu.VMEM((slots, blocks, REACH), f32),
            pltpu.VMEM((5, 2, 2, 2, slots, REACH), f32),
            pltpu.VMEM((3, 2, 2, 2, slots, REACH), f32),
            pltpu.VMEM((2, 2, 2, slots, REACH), f32),
            pltpu.VMEM((8, 8, REACH), f32),
            pltpu.VMEM((8, nc - 1, 8, REACH), f32),
            pltpu.VMEM((16, REACH), f32),
            pltpu.VMEM((3, slots, REACH), f32),
            pltpu.VMEM((8, REACH), f32),
            pltpu.VMEM((nt - 1, 8, REACH), f32),
            pltpu.VMEM((2, slots, REACH), f32),
            dma((2, 2)),
            dma((2, 2)),
            dma((3, 2, slots // GROUP)),
            dma((3, 2, slots // GROUP)),
            dma((8, nc - 1)),
            dma((8, nc - 1)),
            dma((nt - 1,)),
            dma((nt - 1,)),
        ],
        compiler_params=pltpu.CompilerParams(
            collective_id=0, has_side_effects=True, vmem_limit_bytes=48 * 1024 * 1024
        ),
    )(field, noise, arranged(field), arranged(noise), tap_rows(assign))
    return restored(received), restored(recovered)


def solution(mesh):
    placed = (P(None, None, "chan", "tm"), P(None, None, None, "chan", "tm"), P("chan"))
    return jax.shard_map(
        on_device,
        mesh=mesh,
        in_specs=placed,
        out_specs=(P(None, None, "chan", "tm"), P(None, None, "chan", "tm")),
        check_vma=False,
    )
```
